256 devices in a mesh: dp: 32 (over y, x, core), mp: 8 (over z).
Axes of the slice: x: 4, y: 4, z: 8, core: 2. Of those that a mesh axis runs over, the one named last changes fastest.
Arguments:
- tokens_in: bfloat16 [24576, 2048], P(('dp', 'mp')), may hold values from -6 to 6
- pre_act: bfloat16 [24576, 12288], P('dp', 'mp'), may hold values from -8 to 8
- grad_hidden: bfloat16 [24576, 12288], P('dp', 'mp'), may hold values from -0.0625 to 0.0625
- sample_tokens: int32 [32, 3], P('dp'), may hold values from 1 to 256, 672 in all within a row
- block_slot: int32 [8, 12], P('mp'), may hold values from 0 to 31, as said below
- moment: bfloat16 [8, 32, 512, 512], P('mp', 'dp'), may hold values from -0.59765625 to 0.59765625
- second: bfloat16 [8, 32, 512, 512], P('mp', 'dp'), may hold values from 0.019897461 to 0.19921875
- left: float32 [8, 32, 512, 512], P('mp', 'dp'), may hold values from -6 to 6
- right: float32 [8, 32, 512, 512], P('mp', 'dp'), may hold values from -6 to 6
- basis_left: bfloat16 [8, 32, 512, 512], P('mp', 'dp'), as said below
- basis_right: bfloat16 [8, 32, 512, 512], P('mp', 'dp'), as said below
Outputs:
- direction: bfloat16 [2048, 12288], P('dp', 'mp')
- moment_out: bfloat16 [8, 32, 512, 512], P('mp', 'dp')
- second_out: bfloat16 [8, 32, 512, 512], P('mp', 'dp')
- left_out: float32 [8, 32, 512, 512], P('mp', 'dp')
- right_out: float32 [8, 32, 512, 512], P('mp', 'dp')
The draws below stay inside these ranges and needn't reach their ends.
Inputs may be any that keep to these rules, and one draw needn't show every extreme that they name: `block_slot`: slot s belongs to data-group index s. Within each row the entries are distinct, so an owner holds at most 1 block of a hidden-unit shard, and in every row some owner holds exactly 1. Every row lists slot 0 and slot 31. `basis_left`: each [512, 512] matrix is orthogonal up to bfloat16 rounding. `basis_right`: each [512, 512] matrix is orthogonal up to bfloat16 rounding. `sample_tokens`: the counts of each data group sum to 672, and the largest is 256.
All inputs are finite; a program needn't handle non-finite values.
Results may differ from the reference program's by a relative error of at most 0.03.
Values may be sent and summed in bfloat16 or wider, within the bound.
No kernel may reach another device: no remote copies, remote signals or barrier semaphores. Data moves between devices by JAX's collectives and lax.ppermute only.
A program may use at most 128 MiB of HBM per device.

```python
import math
import jax
import jax.numpy as jnp
import numpy as np
from jax import lax

DW = 2048
FFW = 12288
BLK = 512
SEQ = 256
SAMPLES = 3
TOKENS = 24576
VALID = 672
NBC = 12
CAP = 1
SLOTS = 32
N_DP = 32
N_MP = 8


def draw_block_slot(key, part):
    key = jax.random.fold_in(key, 11)
    slot_total = N_DP * CAP

    def one_column(column_key):
        first_key, order_key, mixing_key = jax.random.split(column_key, 3)
        at_start = jax.random.bernoulli(first_key, 0.5)
        heavy_owner = jnp.where(at_start, 0, N_DP - 1).astype(jnp.int32)
        far_slot = jnp.where(at_start, slot_total - 1, 0).astype(jnp.int32)
        shuffled = jax.random.permutation(order_key, slot_total).astype(jnp.int32)
        priority = jnp.where(shuffled // CAP == heavy_owner, 2, jnp.where(shuffled == far_slot, 0, 1))
        others = jnp.argsort(priority, stable=True)
        remaining = shuffled[others][:NBC - CAP]
        listing = jnp.concatenate([heavy_owner * CAP + jnp.arange(CAP).astype(jnp.int32), remaining]).astype(jnp.int32)
        return jax.random.permutation(mixing_key, listing)
    column_keys = jax.random.split(key, N_MP)
    return jax.vmap(one_column)(column_keys)


def rotation_basis(key):
    sign_key, angle_key = jax.random.split(key)
    leading = (N_MP, N_DP * CAP)
    signs = jnp.where(jax.random.bernoulli(sign_key, 0.5, leading + (BLK, 1)), 1.0, -1.0)
    angles = jax.random.uniform(angle_key, leading + (1, BLK // 2), jnp.float32, -math.pi, math.pi)
    rows_idx = jnp.arange(BLK).astype(jnp.int32)[:, None]
    cols_even = 2 * jnp.arange(BLK // 2).astype(jnp.int32)[None, :]
    parity = jnp.zeros((BLK, BLK // 2), jnp.int32)
    for bit_shift in range(BLK.bit_length()):
        parity = parity ^ (rows_idx & cols_even) >> bit_shift & 1
    hadamard_even = (1 - 2 * parity).astype(jnp.float32)
    hadamard_odd = hadamard_even * (1 - 2 * (rows_idx & 1)).astype(jnp.float32)
    cosine = jnp.cos(angles)
    sine = jnp.sin(angles)
    even_cols = cosine * hadamard_even - sine * hadamard_odd
    odd_cols = sine * hadamard_even + cosine * hadamard_odd
    stacked = jnp.stack([even_cols, odd_cols], axis=-1).reshape(leading + (BLK, BLK))
    return (signs * stacked / math.sqrt(BLK)).astype(jnp.bfloat16)


def draw_basis_left(key, part):
    key = jax.random.fold_in(key, 21)
    return rotation_basis(key)


def draw_basis_right(key, part):
    key = jax.random.fold_in(key, 31)
    return rotation_basis(key)


def block_levels(rng, extent, pieces, least, top_value):
    gain, own = 1.0, jax.random.fold_in(rng, 6)
    for axis_at, blocks in pieces:
        draws = jnp.exp(jax.random.uniform(jax.random.fold_in(own, axis_at), (blocks,), jnp.float32, least / len(pieces), top_value / len(pieces)))
        gain = gain * jnp.repeat(draws, extent[axis_at] // blocks).reshape([-1 if axis == axis_at else 1 for axis in range(len(extent))])
    return gain


def profile(amount, total, reach, slope):
    loads = [(1 << 20) // math.isqrt(grade ** slope) + 1 for grade in range(2, amount + 1)]
    surplus, given = total - reach - (amount - 1), [1] * (amount - 1)
    while surplus > 0:
        movable = [i for i in range(amount - 1) if given[i] < reach]
        mass, left = sum([loads[i] for i in movable]), surplus
        for i in movable:
            addition = min(reach - given[i], max(1, left * loads[i] // mass), surplus)
            given[i] = given[i] + addition
            surplus = surplus - addition
    return np.array([reach] + given)


def ragged(key, count, total, limit, slope):
    if count == 2:
        one = jax.random.randint(key, (), max(1, total - limit), min(limit, total - 1) + 1)
        return jnp.stack([one, total - one])
    tallies = jnp.asarray(profile(count, total, limit, slope), jnp.int32)
    pairs = (count - 1) // 2
    source_of, receiver = tallies[1:1 + 2 * pairs:2], tallies[2:2 + 2 * pairs:2]
    room = jnp.minimum(source_of - 1, limit - receiver)
    shifted = jax.random.randint(jax.random.fold_in(key, 1), (pairs,), 0, 1 << 20) % (room + 1)
    tallies = tallies.at[1:1 + 2 * pairs:2].set(source_of - shifted).at[2:2 + 2 * pairs:2].set(receiver + shifted)
    return tallies[jax.random.permutation(jax.random.fold_in(key, 2), count)]


def normal_values(stream_key, extent, width, reach, shards=(), held_as=jnp.bfloat16):
    drawn = jax.random.normal(stream_key, extent, jnp.float32) * width
    if len(shards) > 0:
        drawn = block_levels(stream_key, extent, shards, -0.22, 0.18) * drawn
    return jnp.clip(drawn, min=-reach, max=reach).astype(held_as)


def setup_inputs(seed: int = 0) -> dict:
    splits = jax.random.split(jax.random.key(seed), 12)
    tokens_in = normal_values(splits[0], (TOKENS, DW), 1.0, 6.0, ((0, 256),))
    pre_act = normal_values(splits[1], (TOKENS, FFW), 1.5, 8.0, ((0, 32), (1, 8)))
    grad_hidden = normal_values(splits[2], (TOKENS, FFW), (TOKENS // 3) ** -0.5, 0.0625, ((0, 32), (1, 8)))
    sample_tokens = jax.vmap(lambda own: ragged(own, SAMPLES, VALID, SEQ, 1))(jax.random.split(splits[3], N_DP)).reshape((N_DP, SAMPLES)).astype(jnp.int32)
    block_slot = draw_block_slot(jax.random.fold_in(splits[11], 71), 0)
    moment = normal_values(splits[5], (N_MP, SLOTS, BLK, BLK), 0.1, 0.59765625, ((0, 8), (1, 32)))
    second = jnp.clip(jnp.exp(math.log(0.19921875) - 2.3038113 * jax.random.uniform(splits[6], (N_MP, SLOTS, BLK, BLK), jnp.float32) ** block_levels(splits[6], (N_MP, SLOTS, BLK, BLK), ((0, 8), (1, 32)), -0.2, 0.2)), 0.019897461, 0.19921875).astype(jnp.bfloat16)
    left = normal_values(splits[7], (N_MP, SLOTS, BLK, BLK), 1.0, 6.0, ((0, 8), (1, 32)), jnp.float32)
    right = normal_values(splits[8], (N_MP, SLOTS, BLK, BLK), 1.0, 6.0, ((0, 8), (1, 32)), jnp.float32)
    basis_left = draw_basis_left(jax.random.fold_in(splits[11], 71), 0)
    basis_right = draw_basis_right(jax.random.fold_in(splits[11], 71), 0)
    return {"tokens_in": tokens_in, "pre_act": pre_act, "grad_hidden": grad_hidden, "sample_tokens": sample_tokens, "block_slot": block_slot, "moment": moment, "second": second, "left": left, "right": right, "basis_left": basis_left, "basis_right": basis_right}


momentum_decay = 0.9
factor_decay = 0.95
adam_epsilon = 1e-08

def gelu_slope(values):
    cumulative = 0.5 * (1.0 + lax.erf(values * 0.7071067811865476))
    density = jnp.exp(-0.5 * values * values) * 0.3989422804014327
    return cumulative + values * density

def soap_block(grad, moment, second, left, right, basis_left, basis_right):
    grad_low = grad.astype(jnp.bfloat16)
    moment_new = (momentum_decay * moment.astype(jnp.float32) + (1.0 - momentum_decay) * grad).astype(jnp.bfloat16)
    front = (((0,), (0,)), ((), ()))
    grad_half = lax.dot_general(basis_left, grad_low, front, preferred_element_type=jnp.float32).astype(jnp.bfloat16)
    grad_turned = jnp.dot(grad_half, basis_right, preferred_element_type=jnp.float32)
    moment_half = lax.dot_general(basis_left, moment_new, front, preferred_element_type=jnp.float32).astype(jnp.bfloat16)
    moment_turned = jnp.dot(moment_half, basis_right, preferred_element_type=jnp.float32)
    second_new = factor_decay * second.astype(jnp.float32) + (1.0 - factor_decay) * grad_turned * grad_turned
    scaled = (moment_turned / (jnp.sqrt(second_new) + adam_epsilon)).astype(jnp.bfloat16)
    back_half = jnp.dot(basis_left, scaled, preferred_element_type=jnp.float32).astype(jnp.bfloat16)
    direction = lax.dot_general(back_half, basis_right, (((1,), (1,)), ((), ())), preferred_element_type=jnp.float32).astype(jnp.bfloat16)
    left_new = factor_decay * left + (1.0 - factor_decay) * lax.dot_general(grad_low, grad_low, (((1,), (1,)), ((), ())), preferred_element_type=jnp.float32)
    right_new = factor_decay * right + (1.0 - factor_decay) * lax.dot_general(grad_low, grad_low, front, preferred_element_type=jnp.float32)
    return (direction, moment_new, second_new.astype(jnp.bfloat16), left_new, right_new)

def reference(tokens_in, pre_act, grad_hidden, sample_tokens, block_slot, moment, second, left, right, basis_left, basis_right):
    total_rows = tokens_in.shape[0]
    group_rows = total_rows // N_DP
    inside = jnp.arange(group_rows).astype(jnp.int32)

    def add_group(carry, items):
        rows_x, rows_pre, rows_g, counts = items
        limits = counts[inside // SEQ]
        keep_row = inside % SEQ < limits
        slope_values = gelu_slope(rows_pre.astype(jnp.float32))
        pre_grad = jnp.where(keep_row[:, None], rows_g.astype(jnp.float32) * slope_values, jnp.float32(0.0)).astype(jnp.bfloat16)
        term = lax.dot_general(rows_x, pre_grad, (((0,), (0,)), ((), ())), preferred_element_type=jnp.float32).astype(jnp.bfloat16)
        term = lax.optimization_barrier(term)
        return (carry + term.astype(jnp.float32), None)
    grad_full = lax.scan(add_group, jnp.zeros((DW, FFW), jnp.float32), (tokens_in.reshape(N_DP, group_rows, DW), pre_act.reshape(N_DP, group_rows, FFW), grad_hidden.reshape(N_DP, group_rows, FFW), sample_tokens.astype(jnp.int32)))[0]
    shard_width = FFW // N_MP
    col_blocks = shard_width // BLK
    row_blocks = DW // BLK
    slot_total = moment.shape[1]
    dir_parts = []
    moment_parts = []
    second_parts = []
    left_parts = []
    right_parts = []
    for column in range(N_MP):
        shard = grad_full[:, column * shard_width:(column + 1) * shard_width]
        blocks = shard.reshape(row_blocks, BLK, col_blocks, BLK).transpose(0, 2, 1, 3).reshape(row_blocks * col_blocks, BLK, BLK)
        listing = block_slot[column].astype(jnp.int32)
        matches = listing[None, :] == jnp.arange(slot_total).astype(jnp.int32)[:, None]
        owned = jnp.any(matches, axis=1)
        which = jnp.argmax(matches, axis=1).astype(jnp.int32)
        grads = jnp.where(owned[:, None, None], blocks[which], jnp.float32(0.0))

        def one_slot(items):
            return soap_block(*items)
        results = lax.map(one_slot, (grads, moment[column], second[column], left[column], right[column], basis_left[column], basis_right[column]))
        kept = owned[:, None, None]
        moment_parts.append(jnp.where(kept, results[1], moment[column]))
        second_parts.append(jnp.where(kept, results[2], second[column]))
        left_parts.append(jnp.where(kept, results[3], left[column]))
        right_parts.append(jnp.where(kept, results[4], right[column]))
        picked = results[0][listing]
        dir_parts.append(picked.reshape(row_blocks, col_blocks, BLK, BLK).transpose(0, 2, 1, 3).reshape(DW, shard_width))
    direction = jnp.concatenate(dir_parts, axis=1)
    return (direction, jnp.stack(moment_parts), jnp.stack(second_parts), jnp.stack(left_parts), jnp.stack(right_parts))
```

```python
import functools

import jax
import jax.numpy as jnp
from jax import lax
from jax.experimental import pallas as pl
from jax.experimental.pallas import tpu as pltpu
from jax.sharding import PartitionSpec as P

SEQ = 256
X_CHIPS = 4
Y_CHIPS = 4
CORES = 2
Z_CHIPS = 8
STRIP = 16
CHUNKS = 2

momentum_decay = 0.9
factor_decay = 0.95
adam_epsilon = 1e-08

FRONT = (((0,), (0,)), ((), ()))
BACK = (((1,), (1,)), ((), ()))
VMEM_LIMIT = 48 * 1024 * 1024


def params(*semantics):
    return pltpu.CompilerParams(
        dimension_semantics=semantics or None, vmem_limit_bytes=VMEM_LIMIT
    )


def core_swap():
    return [(i, i ^ 1) for i in range(32)]


def x_shift(k):
    return [(i, (i // 8) * 8 + (i + 2 * k) % 8) for i in range(32)]


def y_shift(k):
    return [(i, (i + 8 * k) % 32) for i in range(32)]


def z_shift(k):
    return [(i, (i + k) % Z_CHIPS) for i in range(Z_CHIPS)]


def gelu_slope(values):
    cumulative = 0.5 * (1.0 + lax.erf(values * 0.7071067811865476))
    density = jnp.exp(-0.5 * values * values) * 0.3989422804014327
    return cumulative + values * density


def pre_grad_kernel(info, pre_ref, grad_ref, out_ref):
    shard_rows, width = pre_ref.shape
    shard = lax.rem(info[0] + pl.program_id(0), Z_CHIPS)
    position = shard * shard_rows + lax.broadcasted_iota(jnp.int32, (shard_rows, width), 0)
    member = position // SEQ
    limits = jnp.where(member == 0, info[1], jnp.where(member == 1, info[2], info[3]))
    keep = position - member * SEQ < limits
    slope = gelu_slope(pre_ref[...].astype(jnp.float32))
    out_ref[...] = jnp.where(keep, grad_ref[...].astype(jnp.float32) * slope, 0.0).astype(
        out_ref.dtype
    )


def make_pre_grad(pre_act, grad_hidden, info):
    rows, width = pre_act.shape
    shard_rows = rows // Z_CHIPS
    rolled = pl.BlockSpec((shard_rows, width), lambda d, info: (lax.rem(info[0] + d, Z_CHIPS), 0))
    return pl.pallas_call(
        pre_grad_kernel,
        grid_spec=pltpu.PrefetchScalarGridSpec(
            num_scalar_prefetch=1,
            grid=(Z_CHIPS,),
            in_specs=[rolled, rolled],
            out_specs=pl.BlockSpec((shard_rows, width), lambda d, info: (d, 0)),
        ),
        out_shape=jax.ShapeDtypeStruct((rows, width), jnp.bfloat16),
        compiler_params=params("arbitrary"),
        cost_estimate=pl.CostEstimate(
            flops=40 * rows * width, bytes_accessed=6 * rows * width, transcendentals=rows * width
        ),
        name="pre_grad",
    )(info, pre_act, grad_hidden)


def partial_kernel(info, *refs):
    shards, (opposite_own, opposite_sib) = refs[:7], refs[7:9]
    grads_own, grads_sib = refs[9:11]
    outs, (rows_own, rows_sib, total) = refs[11:19], refs[19:22]
    shard_rows = opposite_own.shape[0]

    @pl.when(pl.program_id(0) == 0)
    def _():
        places = (0, 1, 2, 3, 5, 6, 7)
        for place, shard in zip(places, shards):
            span = pl.ds(place * shard_rows, shard_rows)
            rows_own[span, :] = shard[pl.ds(0, shard_rows), :]
            rows_sib[span, :] = shard[pl.ds(shard_rows, shard_rows), :]
        span = pl.ds(4 * shard_rows, shard_rows)
        rows_own[span, :] = opposite_own[...]
        rows_sib[span, :] = opposite_sib[...]

    product = lax.dot_general(
        rows_own[...], grads_own[...], FRONT, preferred_element_type=jnp.float32
    )
    product += lax.dot_general(
        rows_sib[...], grads_sib[...], FRONT, preferred_element_type=jnp.float32
    )
    total[...] = product.astype(total.dtype)
    half = total.shape[0] // 2
    piece = half // X_CHIPS
    for k in range(X_CHIPS):
        start = lax.rem(info[1] + k, X_CHIPS) * piece
        outs[k][...] = total[pl.ds(pl.multiple_of(start, piece), piece), :]
    for k in range(Y_CHIPS):
        inner = lax.rem(info[2] + k, Y_CHIPS) * STRIP
        for xx in range(X_CHIPS):
            start = pl.multiple_of(half + xx * piece + inner, STRIP)
            outs[X_CHIPS + k][pl.ds(xx * STRIP, STRIP), :] = total[pl.ds(start, STRIP), :]


def make_partial(info, shards, grads_own, grads_sib):
    depth, width = grads_own.shape
    chunk = shards[0].shape[1]
    tile = 512
    piece = chunk // 2 // X_CHIPS
    whole = lambda a: pl.BlockSpec(a.shape, lambda n, info: (0, 0))
    tiled = lambda rows: pl.BlockSpec((rows, tile), lambda n, info: (0, n))
    return pl.pallas_call(
        partial_kernel,
        grid_spec=pltpu.PrefetchScalarGridSpec(
            num_scalar_prefetch=1,
            grid=(width // tile,),
            in_specs=[whole(s) for s in shards] + [tiled(depth), tiled(depth)],
            out_specs=[tiled(piece)] * 8,
            scratch_shapes=[
                pltpu.VMEM((depth, chunk), jnp.bfloat16),
                pltpu.VMEM((depth, chunk), jnp.bfloat16),
                pltpu.VMEM((chunk, tile), jnp.bfloat16),
            ],
        ),
        out_shape=[jax.ShapeDtypeStruct((piece, width), jnp.bfloat16)] * 8,
        compiler_params=params("arbitrary"),
        cost_estimate=pl.CostEstimate(
            flops=4 * depth * width * chunk,
            bytes_accessed=4 * depth * (width + chunk) + 2 * chunk * width,
            transcendentals=0,
        ),
        name="partial",
    )(info, *shards, grads_own, grads_sib)


def first_sum_kernel(info, *refs):
    a_in, b_in = refs[:4], refs[4:8]
    a_out, b_out = refs[8:12], refs[12:16]
    total_a, total_b = refs[16:18]
    for pieces, total in ((a_in, total_a), (b_in, total_b)):
        value = pieces[0][...].astype(jnp.float32)
        for piece in pieces[1:]:
            value += piece[...].astype(jnp.float32)
        total[...] = value.astype(total.dtype)
    for k in range(4):
        start = pl.multiple_of(lax.rem(info[2] + k, Y_CHIPS) * STRIP, STRIP)
        a_out[k][...] = total_a[pl.ds(start, STRIP), :]
        start = pl.multiple_of(lax.rem(info[1] + k, X_CHIPS) * STRIP, STRIP)
        b_out[k][...] = total_b[pl.ds(start, STRIP), :]


def make_first_sum(info, a_pieces, b_pieces):
    rows, width = a_pieces[0].shape
    vmem = pl.BlockSpec(memory_space=pltpu.VMEM)
    return pl.pallas_call(
        first_sum_kernel,
        in_specs=[pl.BlockSpec(memory_space=pltpu.SMEM)] + [vmem] * 8,
        out_specs=[vmem] * 8,
        scratch_shapes=[pltpu.VMEM((rows, width), jnp.bfloat16)] * 2,
        out_shape=[jax.ShapeDtypeStruct((STRIP, width), jnp.bfloat16)] * 8,
        compiler_params=params(),
        cost_estimate=pl.CostEstimate(
            flops=8 * rows * width, bytes_accessed=20 * rows * width, transcendentals=0
        ),
        name="first_sum",
    )(info, *a_pieces, *b_pieces)


def second_sum_kernel(col_blocks, listing, *refs):
    pieces, out_ref = refs[:-1], refs[-1]
    block = out_ref.shape[2]
    out_ref[...] = jnp.zeros_like(out_ref)
    for r in range(len(pieces) // 4):
        value = pieces[4 * r][...].astype(jnp.float32)
        for piece in pieces[4 * r + 1 : 4 * r + 4]:
            value += piece[...].astype(jnp.float32)
        value = value.astype(out_ref.dtype)
        for c in range(col_blocks):
            out_ref[listing[r * col_blocks + c]] = value[:, c * block : (c + 1) * block]


def make_second_sum(listing, pieces, slots, block):
    width = pieces[0].shape[1]
    vmem = pl.BlockSpec(memory_space=pltpu.VMEM)
    return pl.pallas_call(
        functools.partial(second_sum_kernel, width // block),
        in_specs=[pl.BlockSpec(memory_space=pltpu.SMEM)] + [vmem] * len(pieces),
        out_specs=vmem,
        out_shape=jax.ShapeDtypeStruct((slots, STRIP, block), jnp.bfloat16),
        compiler_params=params(),
        name="second_sum",
    )(listing, *pieces)


def load_grad(strips_ref, grad_ref):
    for y in range(Y_CHIPS):
        for x in range(X_CHIPS):
            for c in range(CORES):
                start = c * 256 + x * 64 + y * STRIP
                grad_ref[pl.ds(start, STRIP), :] = strips_ref[y * 8 + x * 2 + c]


def direction_kernel(
    owned, strips, moment, second, basis_left, basis_right, direction, moment_out, second_out, grad
):
    @pl.when(owned[0] == 0)
    def _():
        moment_out[...] = moment[...]
        second_out[...] = second[...]
        direction[...] = jnp.zeros_like(direction)

    @pl.when(owned[0] != 0)
    def _():
        load_grad(strips, grad)
        left, right, low = basis_left[...], basis_right[...], grad[...]
        fresh = (
            momentum_decay * moment[...].astype(jnp.float32)
            + (1.0 - momentum_decay) * low.astype(jnp.float32)
        ).astype(jnp.bfloat16)
        moment_out[...] = fresh
        dot = functools.partial(lax.dot_general, preferred_element_type=jnp.float32)
        plain = (((1,), (0,)), ((), ()))
        moment_half = dot(left, fresh, FRONT).astype(jnp.bfloat16)
        grad_half = dot(left, low, FRONT).astype(jnp.bfloat16)
        moment_turned = dot(moment_half, right, plain)
        grad_turned = dot(grad_half, right, plain)
        second_new = (
            factor_decay * second[...].astype(jnp.float32)
            + (1.0 - factor_decay) * grad_turned * grad_turned
        )
        second_out[...] = second_new.astype(jnp.bfloat16)
        scaled = (moment_turned / (jnp.sqrt(second_new) + adam_epsilon)).astype(jnp.bfloat16)
        back_half = dot(left, scaled, plain).astype(jnp.bfloat16)
        update = dot(back_half, right, BACK).astype(jnp.bfloat16)
        for y in range(Y_CHIPS):
            for x in range(X_CHIPS):
                for c in range(CORES):
                    start = x * 128 + c * 64 + y * STRIP
                    direction[y * 8 + x * 2 + c] = update[start : start + STRIP, :]


def make_direction(owned, strips, moment, second, basis_left, basis_right):
    block = moment.shape[0]
    vmem = pl.BlockSpec(memory_space=pltpu.VMEM)
    return pl.pallas_call(
        direction_kernel,
        in_specs=[pl.BlockSpec(memory_space=pltpu.SMEM)] + [vmem] * 5,
        out_specs=[vmem] * 3,
        scratch_shapes=[pltpu.VMEM((block, block), jnp.bfloat16)],
        out_shape=[
            jax.ShapeDtypeStruct(strips.shape, jnp.bfloat16),
            jax.ShapeDtypeStruct(moment.shape, jnp.bfloat16),
            jax.ShapeDtypeStruct(second.shape, jnp.bfloat16),
        ],
        compiler_params=params(),
        cost_estimate=pl.CostEstimate(
            flops=12 * block**3, bytes_accessed=16 * block**2, transcendentals=block**2
        ),
        name="direction",
    )(owned, strips, moment, second, basis_left, basis_right)


def factor_kernel(owned, strips, left, right, left_out, right_out, grad):
    @pl.when(owned[0] == 0)
    def _():
        left_out[...] = left[...]
        right_out[...] = right[...]

    @pl.when(owned[0] != 0)
    def _():
        load_grad(strips, grad)
        low = grad[...]
        dot = functools.partial(lax.dot_general, preferred_element_type=jnp.float32)
        left_out[...] = factor_decay * left[...] + (1.0 - factor_decay) * dot(low, low, BACK)
        right_out[...] = factor_decay * right[...] + (1.0 - factor_decay) * dot(low, low, FRONT)


def make_factors(owned, strips, left, right):
    block = left.shape[0]
    vmem = pl.BlockSpec(memory_space=pltpu.VMEM)
    return pl.pallas_call(
        factor_kernel,
        in_specs=[pl.BlockSpec(memory_space=pltpu.SMEM)] + [vmem] * 3,
        out_specs=[vmem] * 2,
        scratch_shapes=[pltpu.VMEM((block, block), jnp.bfloat16)],
        out_shape=[jax.ShapeDtypeStruct(left.shape, jnp.float32)] * 2,
        compiler_params=params(),
        cost_estimate=pl.CostEstimate(
            flops=4 * block**3, bytes_accessed=18 * block**2, transcendentals=0
        ),
        name="factors",
    )(owned, strips, left, right)


def pick_kernel(col_blocks, info, listing, strips, *outs):
    block = strips.shape[2]
    for k in range(Y_CHIPS):
        r = lax.rem(info[2] + k, Y_CHIPS)
        for c in range(col_blocks):
            outs[k][:, c * block : (c + 1) * block] = strips[listing[r * col_blocks + c]]


def make_pick(info, listing, strips, col_blocks):
    vmem = pl.BlockSpec(memory_space=pltpu.VMEM)
    smem = pl.BlockSpec(memory_space=pltpu.SMEM)
    width = strips.shape[2] * col_blocks
    return pl.pallas_call(
        functools.partial(pick_kernel, col_blocks),
        in_specs=[smem, smem, vmem],
        out_specs=[vmem] * Y_CHIPS,
        out_shape=[jax.ShapeDtypeStruct((STRIP, width), jnp.bfloat16)] * Y_CHIPS,
        compiler_params=params(),
        name="pick",
    )(info, listing, strips)


def place_kernel(info, *refs):
    pieces, out_ref = refs[:-1], refs[-1]
    for k in range(Y_CHIPS):
        start = lax.rem(info[2] + Y_CHIPS - k, Y_CHIPS) * STRIP
        out_ref[pl.ds(pl.multiple_of(start, STRIP), STRIP), :] = pieces[k][...]


def make_place(info, pieces):
    vmem = pl.BlockSpec(memory_space=pltpu.VMEM)
    rows, width = pieces[0].shape
    return pl.pallas_call(
        place_kernel,
        in_specs=[pl.BlockSpec(memory_space=pltpu.SMEM)] + [vmem] * Y_CHIPS,
        out_specs=vmem,
        out_shape=jax.ShapeDtypeStruct((rows * Y_CHIPS, width), jnp.bfloat16),
        compiler_params=params(),
        name="place",
    )(info, *pieces)


def ring_gather(starts):
    count = len(starts)
    up, down = list(starts), list(starts)
    gathered = [{0: s} for s in starts]
    for hop in range(1, 4):
        for q in range(count):
            up[q] = lax.ppermute(up[q], "mp", z_shift(1))
            down[q] = lax.ppermute(down[q], "mp", z_shift(-1))
            gathered[q][Z_CHIPS - hop] = up[q]
            gathered[q][hop] = down[q]
    for q in range(count):
        rows = starts[q].shape[0] // 2
        own = lax.ppermute(up[q][:rows], "mp", z_shift(1))
        sib = lax.ppermute(down[q][rows:], "mp", z_shift(-1))
        gathered[q][4] = (own, sib)
    return [[g[d] for d in (0, 1, 2, 3, 5, 6, 7)] + list(g[4]) for g in gathered]


def body(
    tokens_in,
    pre_act,
    grad_hidden,
    sample_tokens,
    block_slot,
    moment,
    second,
    left,
    right,
    basis_left,
    basis_right,
):
    place = lax.axis_index("dp")
    at_x, at_y, core = (place // CORES) % X_CHIPS, place // (CORES * X_CHIPS), place % CORES
    at_z = lax.axis_index("mp")
    block = moment.shape[2]
    slots = lax.axis_size("dp")
    listing = block_slot[0]
    info = jnp.stack([at_z, at_x, at_y, core]).astype(jnp.int32)
    own_slot = jnp.any(listing == place).astype(jnp.int32)[None]

    rows, model_width = tokens_in.shape
    halves = tokens_in.reshape(rows, model_width // block, CORES, block // CORES)
    kept = jnp.where(core == 0, halves[:, :, 0], halves[:, :, 1])
    given = jnp.where(core == 0, halves[:, :, 1], halves[:, :, 0])
    kept, given = kept.reshape(rows, -1), given.reshape(rows, -1)
    taken = lax.ppermute(given, "dp", core_swap())
    chunk = kept.shape[1] // CHUNKS
    starts = [
        jnp.concatenate([kept[:, q * chunk : (q + 1) * chunk], taken[:, q * chunk : (q + 1) * chunk]])
        for q in range(CHUNKS)
    ]

    shard_info = jnp.concatenate([info[:1], sample_tokens[0]])
    grads_own = make_pre_grad(pre_act, grad_hidden, shard_info)
    grads_sib = lax.ppermute(grads_own, "dp", core_swap())

    strips = []
    for shards in ring_gather(starts):
        pieces = make_partial(info, shards, grads_own, grads_sib)
        a_pieces = [pieces[0]] + [lax.ppermute(pieces[k], "dp", x_shift(k)) for k in (1, 2, 3)]
        b_pieces = [pieces[4]] + [lax.ppermute(pieces[4 + k], "dp", y_shift(k)) for k in (1, 2, 3)]
        seconds = make_first_sum(info, a_pieces, b_pieces)
        strips += [seconds[0]] + [lax.ppermute(seconds[k], "dp", y_shift(k)) for k in (1, 2, 3)]
        strips += [seconds[4]] + [lax.ppermute(seconds[4 + k], "dp", x_shift(k)) for k in (1, 2, 3)]
    outgoing = make_second_sum(listing, strips, slots, block)
    grad_strips = lax.all_to_all(outgoing, "dp", split_axis=0, concat_axis=0, tiled=True)

    direction_strips, moment_out, second_out = make_direction(
        own_slot, grad_strips, moment[0, 0], second[0, 0], basis_left[0, 0], basis_right[0, 0]
    )
    arrived = lax.all_to_all(direction_strips, "dp", split_axis=0, concat_axis=0, tiled=True)
    left_out, right_out = make_factors(own_slot, grad_strips, left[0, 0], right[0, 0])
    picked = make_pick(info, listing, arrived, pre_act.shape[1] // block)
    rows_mine = [picked[0]] + [lax.ppermute(picked[k], "dp", y_shift(k)) for k in (1, 2, 3)]
    direction = make_place(info, rows_mine)
    return (
        direction,
        moment_out[None, None],
        second_out[None, None],
        left_out[None, None],
        right_out[None, None],
    )


def solution(mesh):
    in_specs = (
        P(("dp", "mp"), None),
        P("dp", "mp"),
        P("dp", "mp"),
        P("dp", None),
        P("mp", None),
        P("mp", "dp", None, None),
        P("mp", "dp", None, None),
        P("mp", "dp", None, None),
        P("mp", "dp", None, None),
        P("mp", "dp", None, None),
        P("mp", "dp", None, None),
    )
    out_specs = (
        P("dp", "mp"),
        P("mp", "dp", None, None),
        P("mp", "dp", None, None),
        P("mp", "dp", None, None),
        P("mp", "dp", None, None),
    )
    return jax.shard_map(body, mesh=mesh, in_specs=in_specs, out_specs=out_specs, check_vma=False)
```

```python
import functools

import jax
import jax.numpy as jnp
from jax import lax
from jax.experimental import pallas as pl
from jax.experimental.pallas import tpu as pltpu
from jax.sharding import PartitionSpec as P

SEQ = 256
X_CHIPS = 4
Y_CHIPS = 4
CORES = 2
Z_CHIPS = 8
STRIP = 16

momentum_decay = 0.9
factor_decay = 0.95
adam_epsilon = 1e-08

FRONT = (((0,), (0,)), ((), ()))
BACK = (((1,), (1,)), ((), ()))
VMEM_LIMIT = 24 * 1024 * 1024


def params(*semantics):
    return pltpu.CompilerParams(
        dimension_semantics=semantics or None, vmem_limit_bytes=VMEM_LIMIT
    )


def core_swap():
    return [(i, i ^ 1) for i in range(32)]


def x_swap(k):
    return [(i, i ^ (CORES * k)) for i in range(32)]


def y_swap(k):
    return [(i, i ^ (CORES * X_CHIPS * k)) for i in range(32)]


def z_swap(odd):
    pairs = [(i, (i + 1) % Z_CHIPS) for i in range(odd, Z_CHIPS, 2)]
    return pairs + [(j, i) for i, j in pairs]


def gelu_slope(values):
    cumulative = 0.5 * (1.0 + lax.erf(values * 0.7071067811865476))
    density = jnp.exp(-0.5 * values * values) * 0.3989422804014327
    return cumulative + values * density


def pre_grad_kernel(info, pre_ref, grad_ref, out_ref):
    shard_rows, width = pre_ref.shape
    shard = info[pl.program_id(0)]
    position = shard * shard_rows + lax.broadcasted_iota(jnp.int32, (shard_rows, width), 0)
    member = position // SEQ
    limits = jnp.where(member == 0, info[8], jnp.where(member == 1, info[9], info[10]))
    keep = position - member * SEQ < limits
    slope = gelu_slope(pre_ref[...].astype(jnp.float32))
    out_ref[...] = jnp.where(keep, grad_ref[...].astype(jnp.float32) * slope, 0.0).astype(
        out_ref.dtype
    )


def make_pre_grad(pre_act, grad_hidden, info):
    rows, width = pre_act.shape
    shard_rows = rows // Z_CHIPS
    rolled = pl.BlockSpec((shard_rows, width), lambda d, info: (info[d], 0))
    return pl.pallas_call(
        pre_grad_kernel,
        grid_spec=pltpu.PrefetchScalarGridSpec(
            num_scalar_prefetch=1,
            grid=(Z_CHIPS,),
            in_specs=[rolled, rolled],
            out_specs=pl.BlockSpec((shard_rows, width), lambda d, info: (d, 0)),
        ),
        out_shape=jax.ShapeDtypeStruct((rows, width), jnp.bfloat16),
        compiler_params=params("arbitrary"),
        cost_estimate=pl.CostEstimate(
            flops=40 * rows * width, bytes_accessed=6 * rows * width, transcendentals=rows * width
        ),
        name="pre_grad",
    )(info, pre_act, grad_hidden)


def stack_rows(shards, rows):
    for place, shard in enumerate(shards):
        count = shard.shape[0]
        rows[pl.ds(place * count, count), :] = shard[...]


def product_rows(rows, grads, first, m, tile):
    left = pl.ds(pl.multiple_of(m * tile, tile), tile)
    return lax.dot_general(
        rows[:, left],
        grads[pl.ds(first, rows.shape[0]), :],
        FRONT,
        preferred_element_type=jnp.float32,
    )


def gather_kernel(count_own, count_sib, first_own, first_sib, resume, *refs):
    own, sib, refs = refs[:count_own], refs[count_own : count_own + count_sib], refs[count_own + count_sib :]
    grads_own, grads_sib = refs[:2]
    before = refs[2] if resume else None
    total, rows_own, rows_sib, held_sib, sem = refs[-5:]
    depth = held_sib.shape[0]
    copy = pltpu.make_async_copy(grads_sib.at[pl.ds(first_sib, depth), :], held_sib, sem)
    copy.start()
    tile = 512
    if own:
        stack_rows(own, rows_own)
    stack_rows(sib, rows_sib)
    copy.wait()

    def step(m, carry):
        product = product_rows(rows_sib, held_sib, 0, m, tile)
        if own:
            product += product_rows(rows_own, grads_own, first_own, m, tile)
        here = pl.ds(pl.multiple_of(m * tile, tile), tile)
        if resume:
            product += before[here, :].astype(jnp.float32)
        total[here, :] = product.astype(total.dtype)
        return carry

    lax.fori_loop(0, total.shape[0] // tile, step, 0)


def make_gathered(own, sib, grads_own, grads_sib, first_own, first_sib, before=None):
    width = grads_own.shape[1]
    rows, chunk = sib[0].shape
    depth_own, depth_sib = max(len(own), 1) * rows, len(sib) * rows
    vmem = pl.BlockSpec(memory_space=pltpu.VMEM)
    operands = [*own, *sib, grads_own, grads_sib] + ([] if before is None else [before])
    specs = [vmem] * len(operands)
    specs[len(own) + len(sib) + 1] = pl.BlockSpec(memory_space=pl.ANY)
    return pl.pallas_call(
        functools.partial(
            gather_kernel, len(own), len(sib), first_own * rows, first_sib * rows, before is not None
        ),
        in_specs=specs,
        out_specs=vmem,
        out_shape=jax.ShapeDtypeStruct((chunk, width), jnp.bfloat16),
        scratch_shapes=[
            pltpu.VMEM((depth_own, chunk), jnp.bfloat16),
            pltpu.VMEM((depth_sib, chunk), jnp.bfloat16),
            pltpu.VMEM((depth_sib, width), jnp.bfloat16),
            pltpu.SemaphoreType.DMA,
        ],
        input_output_aliases={} if before is None else {len(operands) - 1: 0},
        compiler_params=params(),
        cost_estimate=pl.CostEstimate(
            flops=2 * (len(own) * rows + depth_sib) * width * chunk,
            bytes_accessed=4 * width * chunk,
            transcendentals=0,
        ),
        name="gathered",
    )(*operands)


def partial_kernel(x_first, first, info, *refs):
    rows_own, rows_sib, grads_own, grads_sib, before = refs[:5]
    outs, total, held_sib, sem = refs[5:9], refs[9], refs[10], refs[11]
    depth = held_sib.shape[0]
    copy = pltpu.make_async_copy(grads_sib.at[pl.ds(first, depth), :], held_sib, sem)
    copy.start()
    tile = 512
    half = tile // 2
    piece = half // 4
    m = 0 if x_first else 1
    product = before[pl.ds(m * tile, tile), :].astype(jnp.float32)
    product += product_rows(rows_own, grads_own, first, m, tile)
    copy.wait()
    product += product_rows(rows_sib, held_sib, 0, m, tile)
    total[...] = product.astype(total.dtype)
    for k in range(4):
        for r in range(2):
            if x_first:
                start = r * half + (info[1] ^ k) * piece
                outs[k][pl.ds(r * piece, piece), :] = total[
                    pl.ds(pl.multiple_of(start, piece), piece), :
                ]
            else:
                inner = (info[2] ^ k) * STRIP
                for xx in range(X_CHIPS):
                    start = pl.multiple_of(r * half + xx * piece + inner, STRIP)
                    outs[k][pl.ds(r * piece + xx * STRIP, STRIP), :] = total[pl.ds(start, STRIP), :]


def make_partial(info, rows_own, rows_sib, grads_own, grads_sib, before, first, x_first):
    width = grads_own.shape[1]
    rows = rows_own.shape[0]
    piece = 128
    vmem = pl.BlockSpec(memory_space=pltpu.VMEM)
    specs = [pl.BlockSpec(memory_space=pltpu.SMEM)] + [vmem] * 5
    specs[4] = pl.BlockSpec(memory_space=pl.ANY)
    return pl.pallas_call(
        functools.partial(partial_kernel, x_first, first * rows),
        in_specs=specs,
        out_specs=[vmem] * 4,
        out_shape=[jax.ShapeDtypeStruct((piece, width), jnp.bfloat16)] * 4,
        scratch_shapes=[
            pltpu.VMEM((512, width), jnp.bfloat16),
            pltpu.VMEM((rows, width), jnp.bfloat16),
            pltpu.SemaphoreType.DMA,
        ],
        compiler_params=params(),
        cost_estimate=pl.CostEstimate(
            flops=4 * rows * width * 512, bytes_accessed=6 * width * 512, transcendentals=0
        ),
        name="partial",
    )(info, rows_own, rows_sib, grads_own, grads_sib, before)


def first_sum_kernel(which, info, *refs):
    pieces, outs, total = refs[:4], refs[4:8], refs[8]
    value = pieces[0][...].astype(jnp.float32)
    for piece in pieces[1:]:
        value += piece[...].astype(jnp.float32)
    total[...] = value.astype(total.dtype)
    half = total.shape[0] // 2
    for k in range(4):
        for r in range(2):
            start = pl.multiple_of(r * half + (info[which] ^ k) * STRIP, STRIP)
            outs[k][pl.ds(r * STRIP, STRIP), :] = total[pl.ds(start, STRIP), :]


def make_first_sum(info, pieces, which):
    rows, width = pieces[0].shape
    vmem = pl.BlockSpec(memory_space=pltpu.VMEM)
    return pl.pallas_call(
        functools.partial(first_sum_kernel, which),
        in_specs=[pl.BlockSpec(memory_space=pltpu.SMEM)] + [vmem] * 4,
        out_specs=[vmem] * 4,
        scratch_shapes=[pltpu.VMEM((rows, width), jnp.bfloat16)],
        out_shape=[jax.ShapeDtypeStruct((2 * STRIP, width), jnp.bfloat16)] * 4,
        compiler_params=params(),
        cost_estimate=pl.CostEstimate(
            flops=4 * rows * width, bytes_accessed=10 * rows * width, transcendentals=0
        ),
        name="first_sum",
    )(info, *pieces)


def second_sum_kernel(col_blocks, listing, *refs):
    pieces, out_ref = refs[:-1], refs[-1]
    block = out_ref.shape[2]
    out_ref[...] = jnp.zeros_like(out_ref)
    for q in range(len(pieces) // 4):
        value = pieces[4 * q][...].astype(jnp.float32)
        for piece in pieces[4 * q + 1 : 4 * q + 4]:
            value += piece[...].astype(jnp.float32)
        value = value.astype(out_ref.dtype)
        for r in range(2):
            for c in range(col_blocks):
                out_ref[listing[(2 * q + r) * col_blocks + c]] = value[
                    r * STRIP : (r + 1) * STRIP, c * block : (c + 1) * block
                ]


def make_second_sum(listing, pieces, slots, block):
    width = pieces[0].shape[1]
    vmem = pl.BlockSpec(memory_space=pltpu.VMEM)
    return pl.pallas_call(
        functools.partial(second_sum_kernel, width // block),
        in_specs=[pl.BlockSpec(memory_space=pltpu.SMEM)] + [vmem] * len(pieces),
        out_specs=vmem,
        out_shape=jax.ShapeDtypeStruct((slots, STRIP, block), jnp.bfloat16),
        compiler_params=params(),
        name="second_sum",
    )(listing, *pieces)


def load_grad(strips_ref, grad_ref):
    for y in range(Y_CHIPS):
        for x in range(X_CHIPS):
            for c in range(CORES):
                start = c * 256 + x * 64 + y * STRIP
                grad_ref[pl.ds(start, STRIP), :] = strips_ref[y * 8 + x * 2 + c]


def direction_kernel(
    owned, strips, moment, second, basis_left, basis_right, direction, moment_out, second_out, grad
):
    @pl.when(owned[0] == 0)
    def _():
        moment_out[...] = moment[...]
        second_out[...] = second[...]
        direction[...] = jnp.zeros_like(direction)

    @pl.when(owned[0] != 0)
    def _():
        load_grad(strips, grad)
        left, right, low = basis_left[...], basis_right[...], grad[...]
        fresh = (
            momentum_decay * moment[...].astype(jnp.float32)
            + (1.0 - momentum_decay) * low.astype(jnp.float32)
        ).astype(jnp.bfloat16)
        moment_out[...] = fresh
        dot = functools.partial(lax.dot_general, preferred_element_type=jnp.float32)
        plain = (((1,), (0,)), ((), ()))
        moment_half = dot(left, fresh, FRONT).astype(jnp.bfloat16)
        grad_half = dot(left, low, FRONT).astype(jnp.bfloat16)
        moment_turned = dot(moment_half, right, plain)
        grad_turned = dot(grad_half, right, plain)
        second_new = (
            factor_decay * second[...].astype(jnp.float32)
            + (1.0 - factor_decay) * grad_turned * grad_turned
        )
        second_out[...] = second_new.astype(jnp.bfloat16)
        scaled = (moment_turned / (jnp.sqrt(second_new) + adam_epsilon)).astype(jnp.bfloat16)
        back_half = dot(left, scaled, plain).astype(jnp.bfloat16)
        update = dot(back_half, right, BACK).astype(jnp.bfloat16)
        for y in range(Y_CHIPS):
            for x in range(X_CHIPS):
                for c in range(CORES):
                    start = x * 128 + c * 64 + y * STRIP
                    direction[y * 8 + x * 2 + c] = update[start : start + STRIP, :]


def make_direction(owned, strips, moment, second, basis_left, basis_right):
    block = moment.shape[0]
    vmem = pl.BlockSpec(memory_space=pltpu.VMEM)
    return pl.pallas_call(
        direction_kernel,
        in_specs=[pl.BlockSpec(memory_space=pltpu.SMEM)] + [vmem] * 5,
        out_specs=[vmem] * 3,
        scratch_shapes=[pltpu.VMEM((block, block), jnp.bfloat16)],
        out_shape=[
            jax.ShapeDtypeStruct(strips.shape, jnp.bfloat16),
            jax.ShapeDtypeStruct(moment.shape, jnp.bfloat16),
            jax.ShapeDtypeStruct(second.shape, jnp.bfloat16),
        ],
        compiler_params=params(),
        cost_estimate=pl.CostEstimate(
            flops=12 * block**3, bytes_accessed=16 * block**2, transcendentals=block**2
        ),
        name="direction",
    )(owned, strips, moment, second, basis_left, basis_right)


def factor_kernel(owned, strips, left, right, left_out, right_out, grad):
    @pl.when(owned[0] == 0)
    def _():
        left_out[...] = left[...]
        right_out[...] = right[...]

    @pl.when(owned[0] != 0)
    def _():
        load_grad(strips, grad)
        low = grad[...]
        dot = functools.partial(lax.dot_general, preferred_element_type=jnp.float32)
        left_out[...] = factor_decay * left[...] + (1.0 - factor_decay) * dot(low, low, BACK)
        right_out[...] = factor_decay * right[...] + (1.0 - factor_decay) * dot(low, low, FRONT)


def make_factors(owned, strips, left, right):
    block = left.shape[0]
    vmem = pl.BlockSpec(memory_space=pltpu.VMEM)
    return pl.pallas_call(
        factor_kernel,
        in_specs=[pl.BlockSpec(memory_space=pltpu.SMEM)] + [vmem] * 3,
        out_specs=[vmem] * 2,
        scratch_shapes=[pltpu.VMEM((block, block), jnp.bfloat16)],
        out_shape=[jax.ShapeDtypeStruct(left.shape, jnp.float32)] * 2,
        compiler_params=params(),
        cost_estimate=pl.CostEstimate(
            flops=4 * block**3, bytes_accessed=18 * block**2, transcendentals=0
        ),
        name="factors",
    )(owned, strips, left, right)


def pick_kernel(col_blocks, info, listing, strips, *outs):
    block = strips.shape[2]
    for k in range(Y_CHIPS):
        r = info[2] ^ k
        for c in range(col_blocks):
            outs[k][:, c * block : (c + 1) * block] = strips[listing[r * col_blocks + c]]


def make_pick(info, listing, strips, col_blocks):
    vmem = pl.BlockSpec(memory_space=pltpu.VMEM)
    smem = pl.BlockSpec(memory_space=pltpu.SMEM)
    width = strips.shape[2] * col_blocks
    return pl.pallas_call(
        functools.partial(pick_kernel, col_blocks),
        in_specs=[smem, smem, vmem],
        out_specs=[vmem] * Y_CHIPS,
        out_shape=[jax.ShapeDtypeStruct((STRIP, width), jnp.bfloat16)] * Y_CHIPS,
        compiler_params=params(),
        name="pick",
    )(info, listing, strips)


def place_kernel(info, *refs):
    pieces, out_ref = refs[:-1], refs[-1]
    for k in range(Y_CHIPS):
        start = (info[2] ^ k) * STRIP
        out_ref[pl.ds(pl.multiple_of(start, STRIP), STRIP), :] = pieces[k][...]


def make_place(info, pieces):
    vmem = pl.BlockSpec(memory_space=pltpu.VMEM)
    rows, width = pieces[0].shape
    return pl.pallas_call(
        place_kernel,
        in_specs=[pl.BlockSpec(memory_space=pltpu.SMEM)] + [vmem] * Y_CHIPS,
        out_specs=vmem,
        out_shape=jax.ShapeDtypeStruct((rows * Y_CHIPS, width), jnp.bfloat16),
        compiler_params=params(),
        name="place",
    )(info, *pieces)


def split_kernel(block, tokens, kept, given):
    half = block // CORES
    core = lax.rem(lax.axis_index("dp"), CORES)
    for r in range(tokens.shape[1] // block):
        for ref, side in ((kept, core), (given, 1 - core)):
            start = pl.multiple_of(r * block + side * half, half)
            ref[:, r * half : (r + 1) * half] = tokens[:, pl.ds(start, half)]


def make_split(tokens, block):
    rows, width = tokens.shape
    vmem = pl.BlockSpec(memory_space=pltpu.VMEM)
    return pl.pallas_call(
        functools.partial(split_kernel, block),
        in_specs=[vmem],
        out_specs=[vmem] * 2,
        out_shape=[jax.ShapeDtypeStruct((rows, width // CORES), tokens.dtype)] * 2,
        compiler_params=params(),
        name="split",
    )(tokens)


def body(
    tokens_in,
    pre_act,
    grad_hidden,
    sample_tokens,
    block_slot,
    moment,
    second,
    left,
    right,
    basis_left,
    basis_right,
):
    place = lax.axis_index("dp")
    at_x, at_y, core = (place // CORES) % X_CHIPS, place // (CORES * X_CHIPS), place % CORES
    at_z = lax.axis_index("mp")
    block = moment.shape[2]
    slots = lax.axis_size("dp")
    listing = block_slot[0]
    info = jnp.stack([at_z, at_x, at_y, core]).astype(jnp.int32)
    own_slot = jnp.any(listing == place).astype(jnp.int32)[None]

    kept, given = make_split(tokens_in, block)
    distance = jnp.array([0, 1, 7, 6, 2, 3, 5, 4], jnp.int32)
    order = (at_z + jnp.where(at_z % 2 == 0, distance, Z_CHIPS - distance)) % Z_CHIPS
    shard_info = jnp.concatenate([order, sample_tokens[0]])

    def pass_on(pair, turn):
        return [lax.ppermute(pair[i], "mp", z_swap((i + turn) % 2)) for i in (0, 1)]

    near_own = pass_on([kept, kept], 0)
    taken = lax.ppermute(given, "dp", core_swap())
    taken, shard_info = lax.optimization_barrier((taken, shard_info))
    near_sib = pass_on([taken, taken], 0)
    grads_own = make_pre_grad(pre_act, grad_hidden, shard_info)
    near_own, grads_own = lax.optimization_barrier((near_own, grads_own))
    middle_own = pass_on(near_own, 1)
    grads_sib = lax.ppermute(grads_own, "dp", core_swap())
    middle_sib = pass_on(near_sib, 1)
    far_own = pass_on(middle_own, 0)
    total = make_gathered(
        [kept, *near_own, *middle_own], [taken, *near_sib], grads_own, grads_sib, 0, 0
    )
    middle_sib, total = lax.optimization_barrier((middle_sib, total))
    far_sib = pass_on(middle_sib, 0)
    last_own = lax.ppermute(far_own[0], "mp", z_swap(1))
    total = make_gathered(far_own, middle_sib, grads_own, grads_sib, 5, 3, total)
    far_sib, total = lax.optimization_barrier((far_sib, total))
    last_sib = lax.ppermute(far_sib[1], "mp", z_swap(0))
    total = make_gathered([], far_sib, grads_own, grads_sib, 0, 5, total)

    swaps = (x_swap, y_swap)
    cut = [
        make_partial(info, last_own, last_sib, grads_own, grads_sib, total, 7, q == 0)
        for q in (0, 1)
    ]
    cut = lax.optimization_barrier(cut)
    strips = []
    for q in (0, 1):
        pieces = [cut[q][0]] + [lax.ppermute(cut[q][k], "dp", swaps[q](k)) for k in (2, 1, 3)]
        seconds = make_first_sum(info, pieces, 2 - q)
        strips += [seconds[0]]
        strips += [lax.ppermute(seconds[k], "dp", swaps[1 - q](k)) for k in (2, 1, 3)]
    outgoing = make_second_sum(listing, strips, slots, block)
    grad_strips = lax.all_to_all(outgoing, "dp", split_axis=0, concat_axis=0, tiled=True)

    direction_strips, moment_out, second_out = make_direction(
        own_slot, grad_strips, moment[0, 0], second[0, 0], basis_left[0, 0], basis_right[0, 0]
    )
    arrived = lax.all_to_all(direction_strips, "dp", split_axis=0, concat_axis=0, tiled=True)
    left_out, right_out = make_factors(own_slot, grad_strips, left[0, 0], right[0, 0])
    picked = make_pick(info, listing, arrived, pre_act.shape[1] // block)
    rows_mine = [picked[0]] + [lax.ppermute(picked[k], "dp", y_swap(k)) for k in (1, 2, 3)]
    direction = make_place(info, rows_mine)
    return (
        direction,
        moment_out[None, None],
        second_out[None, None],
        left_out[None, None],
        right_out[None, None],
    )


def solution(mesh):
    in_specs = (
        P(("dp", "mp"), None),
        P("dp", "mp"),
        P("dp", "mp"),
        P("dp", None),
        P("mp", None),
        P("mp", "dp", None, None),
        P("mp", "dp", None, None),
        P("mp", "dp", None, None),
        P("mp", "dp", None, None),
        P("mp", "dp", None, None),
        P("mp", "dp", None, None),
    )
    out_specs = (
        P("dp", "mp"),
        P("mp", "dp", None, None),
        P("mp", "dp", None, None),
        P("mp", "dp", None, None),
        P("mp", "dp", None, None),
    )
    return jax.shard_map(body, mesh=mesh, in_specs=in_specs, out_specs=out_specs, check_vma=False)
```

```python
import functools

import jax
import jax.numpy as jnp
from jax import lax
from jax.experimental import pallas as pl
from jax.experimental.pallas import tpu as pltpu
from jax.sharding import PartitionSpec as P

SEQ = 256
X_CHIPS = 4
Y_CHIPS = 4
CORES = 2
Z_CHIPS = 8
STRIP = 16

momentum_decay = 0.9
factor_decay = 0.95
adam_epsilon = 1e-08

FRONT = (((0,), (0,)), ((), ()))
BACK = (((1,), (1,)), ((), ()))
VMEM_LIMIT = 24 * 1024 * 1024


def params(*semantics):
    return pltpu.CompilerParams(
        dimension_semantics=semantics or None, vmem_limit_bytes=VMEM_LIMIT
    )


def core_swap():
    return [(i, i ^ 1) for i in range(32)]


def x_swap(k):
    return [(i, i ^ (CORES * k)) for i in range(32)]


def y_swap(k):
    return [(i, i ^ (CORES * X_CHIPS * k)) for i in range(32)]


def z_swap(odd):
    pairs = [(i, (i + 1) % Z_CHIPS) for i in range(odd, Z_CHIPS, 2)]
    return pairs + [(j, i) for i, j in pairs]


def gelu_slope(values):
    cumulative = 0.5 * (1.0 + lax.erf(values * 0.7071067811865476))
    density = jnp.exp(-0.5 * values * values) * 0.3989422804014327
    return cumulative + values * density


def pre_grad_kernel(info, pre_ref, grad_ref, out_ref):
    shard_rows, width = pre_ref.shape
    shard = info[pl.program_id(0)]
    position = shard * shard_rows + lax.broadcasted_iota(jnp.int32, (shard_rows, width), 0)
    member = position // SEQ
    limits = jnp.where(member == 0, info[8], jnp.where(member == 1, info[9], info[10]))
    keep = position - member * SEQ < limits
    slope = gelu_slope(pre_ref[...].astype(jnp.float32))
    out_ref[...] = jnp.where(keep, grad_ref[...].astype(jnp.float32) * slope, 0.0).astype(
        out_ref.dtype
    )


def make_pre_grad(pre_act, grad_hidden, info):
    rows, width = pre_act.shape
    shard_rows = rows // Z_CHIPS
    rolled = pl.BlockSpec((shard_rows, width), lambda d, info: (info[d], 0))
    return pl.pallas_call(
        pre_grad_kernel,
        grid_spec=pltpu.PrefetchScalarGridSpec(
            num_scalar_prefetch=1,
            grid=(Z_CHIPS,),
            in_specs=[rolled, rolled],
            out_specs=pl.BlockSpec((shard_rows, width), lambda d, info: (d, 0)),
        ),
        out_shape=jax.ShapeDtypeStruct((rows, width), jnp.bfloat16),
        compiler_params=params("arbitrary"),
        cost_estimate=pl.CostEstimate(
            flops=40 * rows * width, bytes_accessed=6 * rows * width, transcendentals=rows * width
        ),
        name="pre_grad",
    )(info, pre_act, grad_hidden)


def stack_rows(shards, rows):
    for place, shard in enumerate(shards):
        count = shard.shape[0]
        rows[pl.ds(place * count, count), :] = shard[...]


def product_rows(rows, grads, first, m, tile):
    left = pl.ds(pl.multiple_of(m * tile, tile), tile)
    return lax.dot_general(
        rows[:, left],
        grads[pl.ds(first, rows.shape[0]), :],
        FRONT,
        preferred_element_type=jnp.float32,
    )


def gather_kernel(count_own, count_sib, first_own, first_sib, resume, *refs):
    own, sib, refs = refs[:count_own], refs[count_own : count_own + count_sib], refs[count_own + count_sib :]
    grads_own, grads_sib = refs[:2]
    before = refs[2] if resume else None
    total, rows_own, rows_sib, held_sib, sem = refs[-5:]
    depth = held_sib.shape[0]
    copy = pltpu.make_async_copy(grads_sib.at[pl.ds(first_sib, depth), :], held_sib, sem)
    copy.start()
    tile = 512
    if own:
        stack_rows(own, rows_own)
    stack_rows(sib, rows_sib)
    copy.wait()

    def step(m, carry):
        product = product_rows(rows_sib, held_sib, 0, m, tile)
        if own:
            product += product_rows(rows_own, grads_own, first_own, m, tile)
        here = pl.ds(pl.multiple_of(m * tile, tile), tile)
        if resume:
            product += before[here, :].astype(jnp.float32)
        total[here, :] = product.astype(total.dtype)
        return carry

    lax.fori_loop(0, total.shape[0] // tile, step, 0)


def make_gathered(own, sib, grads_own, grads_sib, first_own, first_sib, before=None):
    width = grads_own.shape[1]
    rows, chunk = sib[0].shape
    depth_own, depth_sib = max(len(own), 1) * rows, len(sib) * rows
    vmem = pl.BlockSpec(memory_space=pltpu.VMEM)
    operands = [*own, *sib, grads_own, grads_sib] + ([] if before is None else [before])
    specs = [vmem] * len(operands)
    specs[len(own) + len(sib) + 1] = pl.BlockSpec(memory_space=pl.ANY)
    return pl.pallas_call(
        functools.partial(
            gather_kernel, len(own), len(sib), first_own * rows, first_sib * rows, before is not None
        ),
        in_specs=specs,
        out_specs=vmem,
        out_shape=jax.ShapeDtypeStruct((chunk, width), jnp.bfloat16),
        scratch_shapes=[
            pltpu.VMEM((depth_own, chunk), jnp.bfloat16),
            pltpu.VMEM((depth_sib, chunk), jnp.bfloat16),
            pltpu.VMEM((depth_sib, width), jnp.bfloat16),
            pltpu.SemaphoreType.DMA,
        ],
        input_output_aliases={} if before is None else {len(operands) - 1: 0},
        compiler_params=params(),
        cost_estimate=pl.CostEstimate(
            flops=2 * (len(own) * rows + depth_sib) * width * chunk,
            bytes_accessed=4 * width * chunk,
            transcendentals=0,
        ),
        name="gathered",
    )(*operands)


def partial_kernel(x_first, first, info, *refs):
    rows_own, rows_sib, grads_own, grads_sib, before = refs[:5]
    outs, total, held_sib, sem = refs[5:9], refs[9], refs[10], refs[11]
    depth = held_sib.shape[0]
    copy = pltpu.make_async_copy(grads_sib.at[pl.ds(first, depth), :], held_sib, sem)
    copy.start()
    tile = 512
    half = tile // 2
    piece = half // 4
    m = 0 if x_first else 1
    product = before[pl.ds(m * tile, tile), :].astype(jnp.float32)
    product += product_rows(rows_own, grads_own, first, m, tile)
    copy.wait()
    product += product_rows(rows_sib, held_sib, 0, m, tile)
    total[...] = product.astype(total.dtype)
    for k in range(4):
        for r in range(2):
            if x_first:
                start = r * half + (info[1] ^ k) * piece
                outs[k][pl.ds(r * piece, piece), :] = total[
                    pl.ds(pl.multiple_of(start, piece), piece), :
                ]
            else:
                inner = (info[2] ^ k) * STRIP
                for xx in range(X_CHIPS):
                    start = pl.multiple_of(r * half + xx * piece + inner, STRIP)
                    outs[k][pl.ds(r * piece + xx * STRIP, STRIP), :] = total[pl.ds(start, STRIP), :]


def make_partial(info, rows_own, rows_sib, grads_own, grads_sib, before, first, x_first):
    width = grads_own.shape[1]
    rows = rows_own.shape[0]
    piece = 128
    vmem = pl.BlockSpec(memory_space=pltpu.VMEM)
    specs = [pl.BlockSpec(memory_space=pltpu.SMEM)] + [vmem] * 5
    specs[4] = pl.BlockSpec(memory_space=pl.ANY)
    return pl.pallas_call(
        functools.partial(partial_kernel, x_first, first * rows),
        in_specs=specs,
        out_specs=[vmem] * 4,
        out_shape=[jax.ShapeDtypeStruct((piece, width), jnp.bfloat16)] * 4,
        scratch_shapes=[
            pltpu.VMEM((512, width), jnp.bfloat16),
            pltpu.VMEM((rows, width), jnp.bfloat16),
            pltpu.SemaphoreType.DMA,
        ],
        compiler_params=params(),
        cost_estimate=pl.CostEstimate(
            flops=4 * rows * width * 512, bytes_accessed=6 * width * 512, transcendentals=0
        ),
        name="partial",
    )(info, rows_own, rows_sib, grads_own, grads_sib, before)


def first_sum_kernel(which, info, *refs):
    pieces, outs, total = refs[:4], refs[4:8], refs[8]
    value = pieces[0][...].astype(jnp.float32)
    for piece in pieces[1:]:
        value += piece[...].astype(jnp.float32)
    total[...] = value.astype(total.dtype)
    half = total.shape[0] // 2
    for k in range(4):
        for r in range(2):
            start = pl.multiple_of(r * half + (info[which] ^ k) * STRIP, STRIP)
            outs[k][pl.ds(r * STRIP, STRIP), :] = total[pl.ds(start, STRIP), :]


def make_first_sum(info, pieces, which):
    rows, width = pieces[0].shape
    vmem = pl.BlockSpec(memory_space=pltpu.VMEM)
    return pl.pallas_call(
        functools.partial(first_sum_kernel, which),
        in_specs=[pl.BlockSpec(memory_space=pltpu.SMEM)] + [vmem] * 4,
        out_specs=[vmem] * 4,
        scratch_shapes=[pltpu.VMEM((rows, width), jnp.bfloat16)],
        out_shape=[jax.ShapeDtypeStruct((2 * STRIP, width), jnp.bfloat16)] * 4,
        compiler_params=params(),
        cost_estimate=pl.CostEstimate(
            flops=4 * rows * width, bytes_accessed=10 * rows * width, transcendentals=0
        ),
        name="first_sum",
    )(info, *pieces)


def second_sum_kernel(col_blocks, listing, *refs):
    pieces, out_ref = refs[:-1], refs[-1]
    block = out_ref.shape[2]
    out_ref[...] = jnp.zeros_like(out_ref)
    for q in range(len(pieces) // 4):
        value = pieces[4 * q][...].astype(jnp.float32)
        for piece in pieces[4 * q + 1 : 4 * q + 4]:
            value += piece[...].astype(jnp.float32)
        value = value.astype(out_ref.dtype)
        for r in range(2):
            for c in range(col_blocks):
                out_ref[listing[(2 * q + r) * col_blocks + c]] = value[
                    r * STRIP : (r + 1) * STRIP, c * block : (c + 1) * block
                ]


def make_second_sum(listing, pieces, slots, block):
    width = pieces[0].shape[1]
    vmem = pl.BlockSpec(memory_space=pltpu.VMEM)
    return pl.pallas_call(
        functools.partial(second_sum_kernel, width // block),
        in_specs=[pl.BlockSpec(memory_space=pltpu.SMEM)] + [vmem] * len(pieces),
        out_specs=vmem,
        out_shape=jax.ShapeDtypeStruct((slots, STRIP, block), jnp.bfloat16),
        compiler_params=params(),
        name="second_sum",
    )(listing, *pieces)


def load_grad(strips_ref, grad_ref):
    for y in range(Y_CHIPS):
        for x in range(X_CHIPS):
            for c in range(CORES):
                start = c * 256 + x * 64 + y * STRIP
                grad_ref[pl.ds(start, STRIP), :] = strips_ref[y * 8 + x * 2 + c]


def direction_kernel(
    owned, strips, moment, second, basis_left, basis_right, direction, moment_out, second_out, grad
):
    @pl.when(owned[0] == 0)
    def _():
        moment_out[...] = moment[...]
        second_out[...] = second[...]
        direction[...] = jnp.zeros_like(direction)

    @pl.when(owned[0] != 0)
    def _():
        load_grad(strips, grad)
        left, right, low = basis_left[...], basis_right[...], grad[...]
        fresh = (
            momentum_decay * moment[...].astype(jnp.float32)
            + (1.0 - momentum_decay) * low.astype(jnp.float32)
        ).astype(jnp.bfloat16)
        moment_out[...] = fresh
        dot = functools.partial(lax.dot_general, preferred_element_type=jnp.float32)
        plain = (((1,), (0,)), ((), ()))
        moment_half = dot(left, fresh, FRONT).astype(jnp.bfloat16)
        grad_half = dot(left, low, FRONT).astype(jnp.bfloat16)
        moment_turned = dot(moment_half, right, plain)
        grad_turned = dot(grad_half, right, plain)
        second_new = (
            factor_decay * second[...].astype(jnp.float32)
            + (1.0 - factor_decay) * grad_turned * grad_turned
        )
        second_out[...] = second_new.astype(jnp.bfloat16)
        scaled = (moment_turned / (jnp.sqrt(second_new) + adam_epsilon)).astype(jnp.bfloat16)
        back_half = dot(left, scaled, plain).astype(jnp.bfloat16)
        update = dot(back_half, right, BACK).astype(jnp.bfloat16)
        for y in range(Y_CHIPS):
            for x in range(X_CHIPS):
                for c in range(CORES):
                    start = x * 128 + c * 64 + y * STRIP
                    direction[y * 8 + x * 2 + c] = update[start : start + STRIP, :]


def make_direction(owned, strips, moment, second, basis_left, basis_right):
    block = moment.shape[0]
    vmem = pl.BlockSpec(memory_space=pltpu.VMEM)
    return pl.pallas_call(
        direction_kernel,
        in_specs=[pl.BlockSpec(memory_space=pltpu.SMEM)] + [vmem] * 5,
        out_specs=[vmem] * 3,
        scratch_shapes=[pltpu.VMEM((block, block), jnp.bfloat16)],
        out_shape=[
            jax.ShapeDtypeStruct(strips.shape, jnp.bfloat16),
            jax.ShapeDtypeStruct(moment.shape, jnp.bfloat16),
            jax.ShapeDtypeStruct(second.shape, jnp.bfloat16),
        ],
        compiler_params=params(),
        cost_estimate=pl.CostEstimate(
            flops=12 * block**3, bytes_accessed=16 * block**2, transcendentals=block**2
        ),
        name="direction",
    )(owned, strips, moment, second, basis_left, basis_right)


def factor_kernel(owned, strips, left, right, left_out, right_out, grad):
    @pl.when(owned[0] == 0)
    def _():
        left_out[...] = left[...]
        right_out[...] = right[...]

    @pl.when(owned[0] != 0)
    def _():
        load_grad(strips, grad)
        low = grad[...]
        dot = functools.partial(lax.dot_general, preferred_element_type=jnp.float32)
        left_out[...] = factor_decay * left[...] + (1.0 - factor_decay) * dot(low, low, BACK)
        right_out[...] = factor_decay * right[...] + (1.0 - factor_decay) * dot(low, low, FRONT)


def make_factors(owned, strips, left, right):
    block = left.shape[0]
    vmem = pl.BlockSpec(memory_space=pltpu.VMEM)
    return pl.pallas_call(
        factor_kernel,
        in_specs=[pl.BlockSpec(memory_space=pltpu.SMEM)] + [vmem] * 3,
        out_specs=[vmem] * 2,
        scratch_shapes=[pltpu.VMEM((block, block), jnp.bfloat16)],
        out_shape=[jax.ShapeDtypeStruct(left.shape, jnp.float32)] * 2,
        compiler_params=params(),
        cost_estimate=pl.CostEstimate(
            flops=4 * block**3, bytes_accessed=18 * block**2, transcendentals=0
        ),
        name="factors",
    )(owned, strips, left, right)


def pick_kernel(col_blocks, info, listing, strips, *outs):
    block = strips.shape[2]
    for k in range(Y_CHIPS):
        r = info[2] ^ k
        for c in range(col_blocks):
            outs[k][:, c * block : (c + 1) * block] = strips[listing[r * col_blocks + c]]


def make_pick(info, listing, strips, col_blocks):
    vmem = pl.BlockSpec(memory_space=pltpu.VMEM)
    smem = pl.BlockSpec(memory_space=pltpu.SMEM)
    width = strips.shape[2] * col_blocks
    return pl.pallas_call(
        functools.partial(pick_kernel, col_blocks),
        in_specs=[smem, smem, vmem],
        out_specs=[vmem] * Y_CHIPS,
        out_shape=[jax.ShapeDtypeStruct((STRIP, width), jnp.bfloat16)] * Y_CHIPS,
        compiler_params=params(),
        name="pick",
    )(info, listing, strips)


def place_kernel(info, *refs):
    pieces, out_ref = refs[:-1], refs[-1]
    for k in range(Y_CHIPS):
        start = (info[2] ^ k) * STRIP
        out_ref[pl.ds(pl.multiple_of(start, STRIP), STRIP), :] = pieces[k][...]


def make_place(info, pieces):
    vmem = pl.BlockSpec(memory_space=pltpu.VMEM)
    rows, width = pieces[0].shape
    return pl.pallas_call(
        place_kernel,
        in_specs=[pl.BlockSpec(memory_space=pltpu.SMEM)] + [vmem] * Y_CHIPS,
        out_specs=vmem,
        out_shape=jax.ShapeDtypeStruct((rows * Y_CHIPS, width), jnp.bfloat16),
        compiler_params=params(),
        name="place",
    )(info, *pieces)


def split_kernel(block, tokens, kept, given):
    half = block // CORES
    core = lax.rem(lax.axis_index("dp"), CORES)
    for r in range(tokens.shape[1] // block):
        for ref, side in ((kept, core), (given, 1 - core)):
            start = pl.multiple_of(r * block + side * half, half)
            ref[:, r * half : (r + 1) * half] = tokens[:, pl.ds(start, half)]


def make_split(tokens, block):
    rows, width = tokens.shape
    vmem = pl.BlockSpec(memory_space=pltpu.VMEM)
    return pl.pallas_call(
        functools.partial(split_kernel, block),
        in_specs=[vmem],
        out_specs=[vmem] * 2,
        out_shape=[jax.ShapeDtypeStruct((rows, width // CORES), tokens.dtype)] * 2,
        compiler_params=params(),
        name="split",
    )(tokens)


def body(
    tokens_in,
    pre_act,
    grad_hidden,
    sample_tokens,
    block_slot,
    moment,
    second,
    left,
    right,
    basis_left,
    basis_right,
):
    place = lax.axis_index("dp")
    at_x, at_y, core = (place // CORES) % X_CHIPS, place // (CORES * X_CHIPS), place % CORES
    at_z = lax.axis_index("mp")
    block = moment.shape[2]
    slots = lax.axis_size("dp")
    listing = block_slot[0]
    info = jnp.stack([at_z, at_x, at_y, core]).astype(jnp.int32)
    own_slot = jnp.any(listing == place).astype(jnp.int32)[None]

    kept, given = make_split(tokens_in, block)
    distance = jnp.array([0, 1, 7, 6, 2, 3, 5, 4], jnp.int32)
    order = (at_z + jnp.where(at_z % 2 == 0, distance, Z_CHIPS - distance)) % Z_CHIPS
    shard_info = jnp.concatenate([order, sample_tokens[0]])

    def pass_on(pair, turn):
        return [lax.ppermute(pair[i], "mp", z_swap((i + turn) % 2)) for i in (0, 1)]

    near_own = pass_on([kept, kept], 0)
    taken = lax.ppermute(given, "dp", core_swap())
    taken, shard_info = lax.optimization_barrier((taken, shard_info))
    near_sib = pass_on([taken, taken], 0)
    grads_own = make_pre_grad(pre_act, grad_hidden, shard_info)
    near_own, grads_own = lax.optimization_barrier((near_own, grads_own))
    middle_own = pass_on(near_own, 1)
    grads_sib = lax.ppermute(grads_own, "dp", core_swap())
    middle_sib = pass_on(near_sib, 1)
    far_own = pass_on(middle_own, 0)
    total = make_gathered(
        [kept, *near_own, *middle_own], [taken, *near_sib], grads_own, grads_sib, 0, 0
    )
    middle_sib, total = lax.optimization_barrier((middle_sib, total))
    far_sib = pass_on(middle_sib, 0)
    last_own = lax.ppermute(far_own[0], "mp", z_swap(1))
    total = make_gathered(far_own, middle_sib, grads_own, grads_sib, 5, 3, total)
    far_sib, total = lax.optimization_barrier((far_sib, total))
    last_sib = lax.ppermute(far_sib[1], "mp", z_swap(0))
    total = make_gathered([], far_sib, grads_own, grads_sib, 0, 5, total)

    swaps = (x_swap, y_swap)
    strips = []
    for q in (0, 1):
        pieces = make_partial(info, last_own, last_sib, grads_own, grads_sib, total, 7, q == 0)
        pieces = [pieces[0]] + [lax.ppermute(pieces[k], "dp", swaps[q](k)) for k in (1, 3, 2)]
        seconds = make_first_sum(info, pieces, 2 - q)
        strips += [seconds[0]]
        strips += [lax.ppermute(seconds[k], "dp", swaps[1 - q](k)) for k in (1, 3, 2)]
    outgoing = make_second_sum(listing, strips, slots, block)
    grad_strips = lax.all_to_all(outgoing, "dp", split_axis=0, concat_axis=0, tiled=True)

    direction_strips, moment_out, second_out = make_direction(
        own_slot, grad_strips, moment[0, 0], second[0, 0], basis_left[0, 0], basis_right[0, 0]
    )
    arrived = lax.all_to_all(direction_strips, "dp", split_axis=0, concat_axis=0, tiled=True)
    left_out, right_out = make_factors(own_slot, grad_strips, left[0, 0], right[0, 0])
    picked = make_pick(info, listing, arrived, pre_act.shape[1] // block)
    rows_mine = [picked[0]] + [lax.ppermute(picked[k], "dp", y_swap(k)) for k in (1, 2, 3)]
    direction = make_place(info, rows_mine)
    return (
        direction,
        moment_out[None, None],
        second_out[None, None],
        left_out[None, None],
        right_out[None, None],
    )


def solution(mesh):
    in_specs = (
        P(("dp", "mp"), None),
        P("dp", "mp"),
        P("dp", "mp"),
        P("dp", None),
        P("mp", None),
        P("mp", "dp", None, None),
        P("mp", "dp", None, None),
        P("mp", "dp", None, None),
        P("mp", "dp", None, None),
        P("mp", "dp", None, None),
        P("mp", "dp", None, None),
    )
    out_specs = (
        P("dp", "mp"),
        P("mp", "dp", None, None),
        P("mp", "dp", None, None),
        P("mp", "dp", None, None),
        P("mp", "dp", None, None),
    )
    return jax.shard_map(body, mesh=mesh, in_specs=in_specs, out_specs=out_specs, check_vma=False)
```
